128 devices in a mesh: grp: 8 (over y, z_lo), tp: 16 (over z_hi, x, core).
Axes of the slice: x: 4, y: 4, z: 4 (z_hi: 2, z_lo: 2; z = z_hi * 2 + z_lo), core: 2. Of those that a mesh axis runs over, the one named last changes fastest.
Arguments:
- hidden_rows: bfloat16 [3, 1024, 16384], P(None, 'grp', 'tp'), may hold values from -6 to 6
- join_weight: bfloat16 [3, 16384, 16384], P(None, 'tp', 'grp'), may hold values from -0.02734375 to 0.02734375
- head_weight: bfloat16 [16384, 16384], P('grp', 'tp'), may hold values from -1.5 to 1.5
- teacher_logits: bfloat16 [1024, 16384], P('grp', 'tp'), may hold values from -18 to 260
Outputs:
- joined_rows: bfloat16 [1024, 16384], P('tp', 'grp')
- token_loss: float32 [1024], P('grp')
The draws below stay inside these ranges and needn't reach their ends.
All inputs are finite; a program needn't handle non-finite values.
Results may differ from the reference program's by a relative error of at most 0.014.
Values may be sent and summed in bfloat16 or wider, within the bound.
A program may use at most 128 MiB of HBM per device.

```python
import jax
import jax.numpy as jnp

D = 16384
VOCAB = 16384
TOKENS = 1024


def draw_head_weight(key, part):
    key = jax.random.fold_in(key, 7)
    first_key = jax.random.fold_in(key, 0)
    values = jax.random.normal(first_key, (D, VOCAB), jnp.float32)
    return (jnp.clip(values, -6.0, 6.0) * D ** (-0.5)).astype(jnp.bfloat16)


def draw_teacher_logits(key, part):
    key = jax.random.fold_in(key, 11)
    first_key = jax.random.fold_in(key, 0)
    return jnp.clip(3.0 * jax.random.normal(first_key, (TOKENS, VOCAB), jnp.float32), -18.0, 18.0).astype(jnp.bfloat16)


def level_of(key, shape, cuts, smallest, high):
    def one(position, blocks):
        draws = jax.random.uniform(jax.random.fold_in(jax.random.fold_in(key, 6), position), (blocks,), jnp.float32, smallest / len(cuts), high / len(cuts))
        return jnp.repeat(jnp.exp(draws), shape[position] // blocks).reshape((-1,) + (1,) * (len(shape) - position - 1))

    loudness = one(*cuts[0])
    for cut in cuts[1:]:
        loudness = loudness * one(*cut)
    return loudness


def noise(key, dims, scale, reach, cuts=(), held_as=jnp.bfloat16):
    entries = jax.random.normal(key, dims, jnp.float32) * scale
    if len(cuts) > 0:
        entries = level_of(key, dims, cuts, -0.22, 0.18) * entries
    return jnp.clip(entries, min=-reach, max=reach).astype(held_as)


def setup_inputs(seed: int = 0) -> dict:
    key_of = jax.random.split(jax.random.key(seed), 5)
    hidden_rows = noise(key_of[0], (3, TOKENS, D), 1.0, 6.0, ((1, 8), (2, 16)))
    join_weight = noise(key_of[1], (3, D, D), (3 * D) ** -0.5, 0.02734375, ((1, 16), (2, 8)))
    head_weight = draw_head_weight(jax.random.fold_in(key_of[4], 71), 0)
    teacher_logits = draw_teacher_logits(jax.random.fold_in(key_of[4], 71), 0)
    return {"hidden_rows": hidden_rows, "join_weight": join_weight, "head_weight": head_weight, "teacher_logits": teacher_logits}


def reference(hidden_rows, join_weight, head_weight, teacher_logits):
    joined_sum = jnp.dot(hidden_rows[0], join_weight[0], preferred_element_type=jnp.float32)
    joined_sum = joined_sum + jnp.dot(hidden_rows[1], join_weight[1], preferred_element_type=jnp.float32)
    joined_sum = joined_sum + jnp.dot(hidden_rows[2], join_weight[2], preferred_element_type=jnp.float32)
    joined_rows = joined_sum.astype(jnp.bfloat16)
    draft_logits = jnp.dot(joined_rows, head_weight, preferred_element_type=jnp.float32)
    target_values = teacher_logits.astype(jnp.float32)
    log_target = target_values - jax.scipy.special.logsumexp(target_values, axis=1, keepdims=True)
    log_draft = draft_logits - jax.scipy.special.logsumexp(draft_logits, axis=1, keepdims=True)
    token_loss = jnp.sum(jnp.exp(log_target) * (log_target - log_draft), axis=1)
    return joined_rows, token_loss
```

```python
import jax
import jax.numpy as jnp
from jax import lax
from jax.experimental import pallas as pl
from jax.experimental.pallas import tpu as pltpu
from jax.sharding import PartitionSpec as P

MESH = pl.DeviceIdType.MESH
F32 = jnp.float32
BF16 = jnp.bfloat16

SLOTS = (
    ((0, 0, 0), (0, 0, 1)),
    ((3, 0, 1), (1, 0, 1)),
    ((0, 1, 0), (0, 1, 1)),
    ((3, 0, 0), (1, 0, 0)),
    ((3, 1, 0), (2, 0, 1)),
    ((3, 1, 1), (1, 1, 0)),
    ((1, 1, 1), (2, 0, 0)),
    ((2, 1, 0), (2, 1, 1)),
)
PLACE = {piece: (s, pos) for s, pair in enumerate(SLOTS) for pos, piece in enumerate(pair)}

NSEM = 160


def kernel(
    hid, wj, wh, tl, out_j, out_l,
    W, H, T, X, ACC, S0, R0, S1, R1, Q, S2, R2, JS, LS, RZ, SA, RYA, RYB, SB, RZB, ET, G,
    loc, snd, rcv,
):
    g = lax.axis_index("grp")
    t = lax.axis_index("tp")
    y, zl = g // 2, g % 2
    zh, x, c = t // 8, (t // 2) % 4, t % 2

    def dev(dy=0, dz=0, dx=0, dh=0, dc=0):
        return (
            lax.rem(y + dy, 4) * 2 + lax.rem(zl + dz, 2),
            lax.rem(zh + dh, 2) * 8 + lax.rem(x + dx, 4) * 2 + lax.rem(c + dc, 2),
        )

    def pid(piece):
        dy, dz, half = piece
        return (lax.rem(y + dy, 4) * 2 + lax.rem(zl + dz, 2)) * 2 + half

    keys = {}
    sent = []

    def remote(key, src, dst, **to):
        k = keys.setdefault(key, len(keys))
        return pltpu.make_async_remote_copy(
            src_ref=src, dst_ref=dst, send_sem=snd.at[k], recv_sem=rcv.at[k],
            device_id=dev(**to), device_id_type=MESH,
        )

    def send(key, src, dst, **to):
        copy = remote(key, src, dst, **to)
        copy.start()
        sent.append(copy)

    def arrived(key, dst, **to):
        remote(key, dst, dst, **to).wait_recv()

    def own_rows(half):
        return pltpu.make_async_copy(
            hid.at[:, pl.ds(half * 64, 64), :], X.at[pid((0, 0, half))], loc.at[half]
        )

    loads = [pltpu.make_async_copy(wj.at[l], W.at[l], loc.at[2 + l]) for l in range(3)]
    load_h = pltpu.make_async_copy(wh, H, loc.at[5])
    load_t = pltpu.make_async_copy(tl, T, loc.at[6])
    own_rows(0).start()
    own_rows(1).start()
    for load in loads:
        load.start()
    load_t.start()
    load_h.start()

    peers = (
        [dict(dy=k) for k in (1, 2, 3)] + [dict(dz=1), dict(dc=1), dict(dh=1)]
        + [dict(dx=k) for k in (1, 2, 3)] + [dict(dx=k, dh=1) for k in (1, 2, 3)]
    )
    barrier = pltpu.get_barrier_semaphore()
    for to in peers:
        pl.semaphore_signal(barrier, inc=1, device_id=dev(**to), device_id_type=MESH)
    pl.semaphore_wait(barrier, len(peers))

    def rows(piece, part=None):
        if part is None:
            return X.at[pid(piece)]
        return X.at[pid(piece), :, pl.ds(part * 32, 32), :]

    def send_own(half, way, **to):
        send(("A", way, half), hid.at[:, pl.ds(half * 64, 64), :], rows((0, 0, half)), **to)

    UP, DOWN = dict(dy=1), dict(dy=3)
    send_own(1, "up", **UP)
    send_own(1, "down", **DOWN)
    send_own(0, "z", dz=1)
    send_own(0, "up", **UP)
    send_own(0, "down", **DOWN)
    send_own(1, "z", dz=1)

    def pass_on(name, piece, part, **to):
        send(("A", name), rows(piece, part), rows(piece, part), **to)

    def got(name, piece, part=None):
        arrived(name, rows(piece, part), dy=1)

    def relay_b():
        got(("A", "down", 1), (1, 0, 1))
        pass_on("sb", (1, 0, 1), None, **DOWN)
        got(("A", "up", 1), (3, 0, 1))
        pass_on("zb'", (3, 0, 1), None, dz=1)
        pass_on("zb''", (1, 0, 1), None, dz=1)

    def relay_c():
        got(("A", "z", 0), (0, 1, 0))
        pass_on("za up", (0, 1, 0), None, **UP)
        pass_on("za down", (0, 1, 0), None, **DOWN)

    def relay_d():
        got(("A", "up", 0), (3, 0, 0))
        pass_on("sa up", (3, 0, 0), 0, **UP)
        got(("A", "down", 0), (1, 0, 0))
        pass_on("sa down", (1, 0, 0), 1, **DOWN)

    def relay_e():
        got(("A", "za up"), (3, 1, 0))
        pass_on("zsa up", (3, 1, 0), 0, **UP)

    def relay_f():
        got(("A", "zb'"), (3, 1, 1))
        pass_on("zsb", (3, 1, 1), None, **UP)

    def relay_g():
        got(("A", "za down"), (1, 1, 0))
        pass_on("zsa down", (1, 1, 0), 1, **DOWN)

    def wait_rows(s):
        if s == 0:
            own_rows(0).wait()
            own_rows(1).wait()
            for load in loads:
                load.wait()
        if s == 2:
            got(("A", "z", 1), (0, 1, 1))
        if s == 4:
            got(("A", "sb"), (2, 0, 1))
        if s == 6:
            got(("A", "zb''"), (1, 1, 1))
            got(("A", "sa up"), (2, 0, 0), 0)
            got(("A", "sa down"), (2, 0, 0), 1)
        if s == 7:
            got(("A", "zsa up"), (2, 1, 0), 0)
            got(("A", "zsa down"), (2, 1, 0), 1)
            got(("A", "zsb"), (2, 1, 1))

    def st0(s):
        wait_rows(s)
        p0, p1 = pid(SLOTS[s][0]), pid(SLOTS[s][1])

        def joined(col):
            total = None
            for l in range(3):
                a = jnp.concatenate([X[p0, l], X[p1, l]], axis=0)
                part = jnp.dot(a, W[l, :, pl.ds(pl.multiple_of(col, 512), 512)], preferred_element_type=F32)
                total = part if total is None else total + part
            return total

        def theirs(k, carry):
            S0[s, :, pl.ds(pl.multiple_of(k * 512, 512), 512)] = joined((1 - c) * 1024 + k * 512).astype(BF16)
            return carry

        def mine(k, carry):
            ACC[s, :, pl.ds(pl.multiple_of(k * 512, 512), 512)] = joined(c * 1024 + k * 512)
            return carry

        lax.fori_loop(0, 2, theirs, 0)
        send(("B0", s), S0.at[s], R0.at[s], dc=1)
        lax.fori_loop(0, 2, mine, 0)

    def st1(s):
        arrived(("B0", s), R0.at[s], dc=1)
        for j in (2, 1, 3, 0):
            cols = pl.ds(pl.multiple_of(lax.rem(x + j, 4) * 256, 256), 256)
            v = ACC[s, :, cols] + R0[s, :, cols].astype(F32)
            if j:
                S1[s, j - 1] = v.astype(BF16)
                send(("B1", s, j), S1.at[s, j - 1], R1.at[s, j - 1], dx=j)
            else:
                Q[s] = v

    def st2(s):
        v = Q[s]
        for j in (1, 3, 2):
            arrived(("B1", s, j), R1.at[s, j - 1], dx=j)
            v = v + R1[s, j - 1].astype(F32)
        S2[s] = v.astype(BF16)
        send(("B2", s), S2.at[s], R2.at[s], dh=1)

    def st3(s):
        arrived(("B2", s), R2.at[s], dh=1)
        JS[s, c, x] = (S2[s].astype(F32) + R2[s].astype(F32)).astype(BF16)
        for j in (2, 1, 3):
            send(("C1", s, j), JS.at[s, c, x], JS.at[s, c, x], dx=j)

    def st4(s):
        for j in (1, 3, 2):
            arrived(("C1", s, j), JS.at[s, c, lax.rem(x + 4 - j, 4)], dx=j)
        send(("C0", s), JS.at[s, c], JS.at[s, c], dc=1)

    def st5(s):
        if s == 0:
            load_h.wait()
        arrived(("C0", s), JS.at[s, 1 - c], dc=1)

        def head(k, carry):
            cols = pl.ds(pl.multiple_of(k * 256, 256), 256)
            a = jnp.concatenate([JS[s, i, j] for i in range(2) for j in range(4)], axis=1)
            LS[s, :, cols] = jnp.dot(a, H[:, cols], preferred_element_type=F32).astype(BF16)
            return carry

        lax.fori_loop(0, 4, head, 0)

    def logits(piece):
        s, pos = PLACE[piece]
        return LS.at[s, pl.ds(pos * 64, 64), :]

    def value(piece):
        s, pos = PLACE[piece]
        return LS[s, pos * 64 : pos * 64 + 64, :].astype(F32)

    def st6(s):
        for piece in SLOTS[s]:
            dy, dz, half = piece
            if half == 0 and dz == 1:
                send(("DZ", dy), logits(piece), RZ.at[dy], dz=1)
            if half == 1 and dy != 0:
                send(("DYB", dz, dy), logits(piece), RYB.at[dz, dy - 1], dy=dy)

    def over_z(dy):
        arrived(("DZ", dy), RZ.at[dy], dz=1)
        SA[dy - 1] = (value((dy, 0, 0)) + RZ[dy].astype(F32)).astype(BF16)
        send(("DYA", dy), SA.at[dy - 1], RYA.at[dy - 1], dy=dy)

    def over_y():
        v = value((0, 1, 1))
        for dy in (1, 3, 2):
            arrived(("DYB", 1, dy), RYB.at[1, dy - 1], dy=dy)
            v = v + RYB[1, dy - 1].astype(F32)
        SB[...] = v.astype(BF16)
        send(("DZB",), SB, RZB, dz=1)

    def teacher_stats():
        load_t.wait()
        v = T[...].astype(F32)
        top = jnp.max(v, axis=1, keepdims=True)
        e = jnp.exp(v - top)
        ET[...] = e
        return top, jnp.sum(e, axis=1, keepdims=True)

    def finish(target_max, target_sum):
        va = value((0, 0, 0))
        arrived(("DZ", 0), RZ.at[0], dz=1)
        va = va + RZ[0].astype(F32)
        for dy in (1, 3, 2):
            arrived(("DYA", dy), RYA.at[dy - 1], dy=dy)
            va = va + RYA[dy - 1].astype(F32)
        vb = value((0, 0, 1))
        for dy in (1, 3, 2):
            arrived(("DYB", 0, dy), RYB.at[0, dy - 1], dy=dy)
            vb = vb + RYB[0, dy - 1].astype(F32)
        arrived(("DZB",), RZB, dz=1)
        vb = vb + RZB[...].astype(F32)
        draft = jnp.concatenate([va, vb], axis=0)
        draft_max = jnp.max(draft, axis=1, keepdims=True)
        shifted = draft - draft_max
        draft_sum = jnp.sum(jnp.exp(shifted), axis=1, keepdims=True)
        cross = jnp.sum(ET[...] * ((T[...].astype(F32) - target_max) - shifted), axis=1, keepdims=True)
        lane = lax.broadcasted_iota(jnp.int32, (128, 128), 1)
        table = jnp.zeros((128, 128), F32)
        for k, column in enumerate((target_max, target_sum, draft_max, draft_sum, cross)):
            table = jnp.where(lane == k, column, table)
        G[t] = jnp.transpose(table)[0:8, :]
        send(("E0",), G.at[t], G.at[t], dc=1)
        pair = pl.ds((t // 2) * 2, 2)
        arrived(("E0",), G.at[t], dc=1)
        for k, to in enumerate([dict(dx=j, dh=1) for j in (2, 1, 3)] + [dict(dh=1)] + [dict(dx=j) for j in (2, 1, 3)]):
            send(("E1", k), G.at[pair], G.at[pair], **to)
        for k in (4, 5, 6, 0, 1, 2, 3):
            arrived(("E1", k), G.at[pair], dh=1)
        tm, ts, dm, ds, cr = (G[:, k, :] for k in range(5))
        tm_all = jnp.max(tm, axis=0, keepdims=True)
        dm_all = jnp.max(dm, axis=0, keepdims=True)
        tw = jnp.exp(tm - tm_all)
        ts_all = jnp.sum(ts * tw, axis=0, keepdims=True)
        ds_all = jnp.sum(ds * jnp.exp(dm - dm_all), axis=0, keepdims=True)
        cr_all = jnp.sum(tw * (cr + ((tm - tm_all) - (dm - dm_all)) * ts), axis=0, keepdims=True)
        out_l[...] = cr_all / ts_all - jnp.log(ts_all) + jnp.log(ds_all)

    def joined_out():
        place = 0
        for s in range(8):
            for pos in range(2):
                place = place + jnp.where(pid(SLOTS[s][pos]) == t, s * 2 + pos, 0)
        for i in range(2):
            for j in range(4):
                col = (i * 4 + j) * 256
                out_j[:, col : col + 256] = JS[place // 2, i, j, pl.ds(pl.multiple_of((place % 2) * 64, 64), 64), :]

    st0(0)
    st1(0)
    tmax, tsum = teacher_stats()
    relay_b()
    relay_c()
    st0(1)
    st2(0)
    st1(1)
    st3(0)
    st2(1)
    st4(0)
    st3(1)
    st5(0)
    relay_d()
    st0(2)
    st4(1)
    st1(2)
    st0(3)
    st5(1)
    st1(3)
    st2(2)
    st2(3)
    relay_e()
    st0(4)
    st3(2)
    st1(4)
    st3(3)
    relay_f()
    st4(2)
    st2(4)
    st4(3)
    st5(2)
    st5(3)
    st3(4)
    relay_g()
    st0(5)
    st4(4)
    for s in (2, 1, 3):
        st6(s)
    st1(5)
    st5(4)
    st6(4)
    st2(5)
    over_z(3)
    st0(6)
    st0(7)
    st1(6)
    st3(5)
    st1(7)
    st4(5)
    st5(5)
    st6(5)
    st2(6)
    over_z(1)
    st2(7)
    st3(6)
    st3(7)
    st4(6)
    st4(7)
    st5(6)
    st6(6)
    st5(7)
    st6(7)
    over_z(2)
    over_y()
    joined_out()
    finish(tmax, tsum)
    for copy in sent:
        copy.wait_send()
    assert len(keys) <= NSEM, len(keys)


def local(hidden_rows, join_weight, head_weight, teacher_logits):
    vmem = pltpu.VMEM
    joined, loss = pl.pallas_call(
        kernel,
        out_shape=(jax.ShapeDtypeStruct((64, 2048), BF16), jax.ShapeDtypeStruct((1, 128), F32)),
        in_specs=[pl.BlockSpec(memory_space=pl.ANY)] * 4,
        out_specs=[pl.BlockSpec(memory_space=pltpu.VMEM)] * 2,
        scratch_shapes=[
            vmem((3, 1024, 2048), BF16),
            vmem((2048, 1024), BF16),
            vmem((128, 1024), BF16),
            vmem((16, 3, 64, 1024), BF16),
            vmem((8, 128, 1024), F32),
            vmem((8, 128, 1024), BF16),
            vmem((8, 128, 1024), BF16),
            vmem((8, 3, 128, 256), BF16),
            vmem((8, 3, 128, 256), BF16),
            vmem((8, 128, 256), F32),
            vmem((8, 128, 256), BF16),
            vmem((8, 128, 256), BF16),
            vmem((8, 2, 4, 128, 256), BF16),
            vmem((8, 128, 1024), BF16),
            vmem((4, 64, 1024), BF16),
            vmem((3, 64, 1024), BF16),
            vmem((3, 64, 1024), BF16),
            vmem((2, 3, 64, 1024), BF16),
            vmem((64, 1024), BF16),
            vmem((64, 1024), BF16),
            vmem((128, 1024), F32),
            vmem((16, 8, 128), F32),
            pltpu.SemaphoreType.DMA((7,)),
            pltpu.SemaphoreType.DMA((NSEM,)),
            pltpu.SemaphoreType.DMA((NSEM,)),
        ],
        compiler_params=pltpu.CompilerParams(
            collective_id=0, has_side_effects=True, vmem_limit_bytes=60 * 1024 * 1024
        ),
        cost_estimate=pl.CostEstimate(flops=17179869184, bytes_accessed=18350080, transcendentals=262144),
    )(hidden_rows, join_weight, head_weight, teacher_logits)
    return joined, loss.reshape(128)


def solution(mesh):
    in_specs = (P(None, "grp", "tp"), P(None, "tp", "grp"), P("grp", "tp"), P("grp", "tp"))
    out_specs = (P("tp", "grp"), P("grp"))
    return jax.shard_map(local, mesh=mesh, in_specs=in_specs, out_specs=out_specs, check_vma=False)
```

```python
import jax
import jax.numpy as jnp
from jax import lax
from jax.experimental import pallas as pl
from jax.experimental.pallas import tpu as pltpu
from jax.sharding import PartitionSpec as P

MESH = pl.DeviceIdType.MESH
F32 = jnp.float32
BF16 = jnp.bfloat16

SLOTS = (
    ((0, 0, 0), (0, 0, 1)),
    ((3, 0, 1), (1, 0, 1)),
    ((0, 1, 0), (3, 0, 0)),
    ((1, 1, 0), (3, 1, 1)),
    ((2, 0, 0), (2, 0, 1)),
    ((1, 1, 1), (2, 1, 1)),
    ((2, 1, 0), (1, 0, 0)),
    ((0, 1, 1), (3, 1, 0)),
)
WIDE = (7,)
DIRECT = (
    (3, 1, 0),
    (3, 0, 0),
    (1, 0, 0),
    (1, 1, 0),
    (2, 1, 0),
    (2, 0, 0),
)
PLACE = {piece: (s, pos) for s, slot in enumerate(SLOTS) for pos, piece in enumerate(slot)}

START = (
    ("up", (0, 0, 1), None),
    ("down", (0, 0, 1), None),
    ("z", (0, 0, 0), None),
    ("up", (0, 0, 0), None),
    ("down", (0, 0, 0), 0),
    ("z", (0, 0, 1), 0),
)
LATER = {
    "up": (("up", (0, 1, 0), 0), ("up", (3, 0, 0), None), ("up", (3, 1, 1), None), ("up", (0, 1, 0), 1)),
    "down": (("down", (0, 1, 0), None), ("down", (1, 0, 1), None), ("down", (1, 1, 0), None), ("down", (0, 0, 0), 1)),
    "z": (("z", (3, 0, 1), 0), ("z", (3, 0, 1), 1), ("z", (1, 0, 1), 0), ("z", (1, 0, 1), 1), ("z", (0, 0, 1), 1)),
}
TO = {"up": dict(dy=1), "down": dict(dy=3), "z": dict(dz=1)}


def lands(copy):
    way, (dy, dz, half), _ = copy
    return (dy + {"up": 3, "down": 1, "z": 0}[way]) % 4, dz ^ (way == "z"), half


COPIES = START + sum(LATER.values(), ())
CROSS = ((2, 1), (1, 1), (3, 1), (0, 1), (2, 0), (1, 0), (3, 0))
NSEM = 96
POOL = 40


def kernel(
    hid, wj, wh, tl, out_j, out_l,
    W, H, T, X, ACC, S0, R0, S1, R1, Q, S2, R2, JS, S8, R8, J8, LS, RZ, SA, RYA, RYB, SB, RZB, RD,
    ET, TAB, G, loc, snd, rcv,
):
    g = lax.axis_index("grp")
    t = lax.axis_index("tp")
    y, zl = g // 2, g % 2
    zh, x, c = t // 8, (t // 2) % 4, t % 2

    def dev(dy=0, dz=0, dx=0, dh=0, dc=0):
        return (
            lax.rem(y + dy, 4) * 2 + lax.rem(zl + dz, 2),
            lax.rem(zh + dh, 2) * 8 + lax.rem(x + dx, 4) * 2 + lax.rem(c + dc, 2),
        )

    def pid(piece):
        dy, dz, half = piece
        return (lax.rem(y + dy, 4) * 2 + lax.rem(zl + dz, 2)) * 2 + half

    keys = {}
    sent = []

    def remote(key, src, dst, turn, **to):
        k = keys.setdefault(key, len(keys))
        return pltpu.make_async_remote_copy(
            src_ref=src, dst_ref=dst, send_sem=snd.at[turn], recv_sem=rcv.at[k],
            device_id=dev(**to), device_id_type=MESH,
        )

    def send(key, src, dst, **to):
        if len(sent) >= POOL:
            sent[-POOL].wait_send()
        copy = remote(key, src, dst, len(sent) % POOL, **to)
        copy.start()
        sent.append(copy)

    def arrived(key, dst, **to):
        remote(key, dst, dst, 0, **to).wait_recv()

    def own_rows(half):
        return pltpu.make_async_copy(
            hid.at[:, pl.ds(half * 64, 64), :], X.at[pid((0, 0, half))], loc.at[half]
        )

    loads = [pltpu.make_async_copy(wj.at[l], W.at[l], loc.at[2 + l]) for l in range(3)]
    load_h = pltpu.make_async_copy(wh, H, loc.at[5])
    load_t = pltpu.make_async_copy(tl, T, loc.at[6])

    peers = (
        [dict(dy=k) for k in (1, 2, 3)] + [dict(dz=1), dict(dc=1)]
        + [dict(dx=k, dh=h) for k, h in CROSS] + [dict(dy=k, dz=1) for k in (1, 2, 3)]
    )
    barrier = pltpu.get_barrier_semaphore()
    for to in peers:
        pl.semaphore_signal(barrier, inc=1, device_id=dev(**to), device_id_type=MESH)
    own_rows(0).start()
    own_rows(1).start()
    for load in loads:
        load.start()
    load_t.start()
    load_h.start()
    pl.semaphore_wait(barrier, len(peers))

    def rows(piece, part=None):
        if part is None:
            return X.at[pid(piece)]
        return X.at[pid(piece), :, pl.ds(part * 32, 32), :]

    waited = set()

    def need(piece, part=None):
        for copy in COPIES:
            if lands(copy) == piece and copy not in waited and (part is None or copy[2] in (None, part)):
                waited.add(copy)
                arrived(copy, rows(piece, copy[2]), **TO[copy[0]])

    def move(copy):
        way, piece, part = copy
        if piece[:2] == (0, 0):
            first, count = (piece[2] * 64, 64) if part is None else (piece[2] * 64 + part * 32, 32)
            src = hid.at[:, pl.ds(first, count), :]
        else:
            need(piece, part)
            src = rows(piece, part)
        send(copy, src, rows(piece, part), **TO[way])

    def onward(way, k):
        move(LATER[way][k])

    for copy in START:
        move(copy)

    def size(s):
        return 64 * len(SLOTS[s])

    def top(s):
        return pl.ds(0, size(s))

    def st0(s):
        for piece in SLOTS[s]:
            need(piece)
        if s == 0:
            own_rows(0).wait()
            own_rows(1).wait()
            for load in loads:
                load.wait()
        places = [pid(piece) for piece in SLOTS[s]]

        def joined(col):
            total = None
            for l in range(3):
                a = jnp.concatenate([X[p, l] for p in places], axis=0)
                part = jnp.dot(a, W[l, :, pl.ds(pl.multiple_of(col, 512), 512)], preferred_element_type=F32)
                total = part if total is None else total + part
            return total

        def theirs(k, carry):
            S0[s, top(s), pl.ds(pl.multiple_of(k * 512, 512), 512)] = joined((1 - c) * 1024 + k * 512).astype(BF16)
            return carry

        def mine(k, carry):
            ACC[s, top(s), pl.ds(pl.multiple_of(k * 512, 512), 512)] = joined(c * 1024 + k * 512)
            return carry

        lax.fori_loop(0, 2, theirs, 0)
        send(("B0", s), S0.at[s, top(s)], R0.at[s, top(s)], dc=1)
        lax.fori_loop(0, 2, mine, 0)

    def pair_sum(s, first, count):
        cols = pl.ds(pl.multiple_of(first, count), count)
        return ACC[s, top(s), cols] + R0[s, top(s), cols].astype(F32)

    def st1(s):
        arrived(("B0", s), R0.at[s, top(s)], dc=1)
        if s in WIDE:
            w = WIDE.index(s)
            for j, (dx, dh) in enumerate(CROSS):
                S8[w, j, top(s)] = pair_sum(s, (lax.rem(zh + dh, 2) * 4 + lax.rem(x + dx, 4)) * 128, 128).astype(BF16)
                send(("B1", s), S8.at[w, j, top(s)], R8.at[w, j, top(s)], dx=dx, dh=dh)
            Q[s, top(s), 0:128] = pair_sum(s, (zh * 4 + x) * 128, 128)
            return
        for j in (2, 1, 3):
            S1[s, j - 1, top(s)] = pair_sum(s, lax.rem(x + j, 4) * 256, 256).astype(BF16)
            send(("B1", s), S1.at[s, j - 1, top(s)], R1.at[s, j - 1, top(s)], dx=j)
        Q[s, top(s)] = pair_sum(s, x * 256, 256)

    def st2(s):
        if s in WIDE:
            w = WIDE.index(s)
            v = Q[s, top(s), 0:128]
            arrived(("B1", s), R8.at[w, :, top(s)], dx=1)
            for j in range(7):
                v = v + R8[w, j, top(s)].astype(F32)
            mine = J8.at[w, c, zh * 4 + x, top(s)]
            mine[...] = v.astype(BF16)
            for j, (dx, dh) in enumerate(CROSS):
                send(("C1", s), mine, mine, dx=dx, dh=dh)
            return
        v = Q[s, top(s)]
        arrived(("B1", s), R1.at[s, :, top(s)], dx=1)
        for j in (1, 2, 3):
            v = v + R1[s, j - 1, top(s)].astype(F32)
        S2[s, top(s)] = v.astype(BF16)
        send(("B2", s), S2.at[s, top(s)], R2.at[s, top(s)], dh=1)

    def st3(s):
        arrived(("B2", s), R2.at[s, top(s)], dh=1)
        mine = JS.at[s, c, x, top(s)]
        mine[...] = (S2[s, top(s)].astype(F32) + R2[s, top(s)].astype(F32)).astype(BF16)
        for j in (2, 1, 3):
            send(("C1", s), mine, mine, dx=j)

    def blocks(s):
        if s in WIDE:
            return J8, WIDE.index(s), 8
        return JS, s, 4

    def st4(s):
        buf, k, parts = blocks(s)
        arrived(("C1", s), buf.at[k, c, pl.ds(0, parts - 1), top(s)], dx=1)
        send(("C0", s), buf.at[k, c, :, top(s)], buf.at[k, c, :, top(s)], dc=1)

    def st5(s):
        if s == 0:
            load_h.wait()
        buf, k, parts = blocks(s)
        arrived(("C0", s), buf.at[k, 1 - c, :, top(s)], dc=1)
        cuts = [(i, j) for i in range(2) for j in range(parts)]

        def head(n, carry):
            cols = pl.ds(pl.multiple_of(n * 256, 256), 256)
            a = jnp.concatenate([buf[k, i, j, top(s)] for i, j in cuts], axis=1)
            LS[s, top(s), cols] = jnp.dot(a, H[:, cols], preferred_element_type=F32).astype(BF16)
            return carry

        lax.fori_loop(0, 4, head, 0)

    def logits(piece):
        s, pos = PLACE[piece]
        return LS.at[s, pl.ds(pos * 64, 64), :]

    def value(piece):
        s, pos = PLACE[piece]
        return LS[s, pos * 64 : pos * 64 + 64, :].astype(F32)

    def st6(s):
        for piece in SLOTS[s]:
            dy, dz, half = piece
            if piece in DIRECT:
                send(("DD", piece), logits(piece), RD.at[DIRECT.index(piece)], dy=dy, dz=dz)
            elif half == 0 and dz == 1:
                send(("DZ", dy), logits(piece), RZ.at[dy], dz=1)
            elif half == 1 and dy != 0:
                send(("DYB", dz, dy), logits(piece), RYB.at[dz, dy - 1], dy=dy)
        for pos, piece in enumerate(SLOTS[s]):
            buf, k, parts = blocks(s)

            @pl.when(pid(piece) == t)
            def _():
                width = 1024 // parts
                for i in range(2):
                    for j in range(parts):
                        col = i * 1024 + j * width
                        out_j[:, col : col + width] = buf[k, i, j, pos * 64 : pos * 64 + 64, :]

    def over_z(dy):
        arrived(("DZ", dy), RZ.at[dy], dz=1)
        SA[dy - 1] = (value((dy, 0, 0)) + RZ[dy].astype(F32)).astype(BF16)
        send(("DYA", dy), SA.at[dy - 1], RYA.at[dy - 1], dy=dy)

    def over_y():
        v = value((0, 1, 1))
        for dy in (1, 3, 2):
            if (dy, 1, 1) not in DIRECT:
                arrived(("DYB", 1, dy), RYB.at[1, dy - 1], dy=dy)
                v = v + RYB[1, dy - 1].astype(F32)
        SB[...] = v.astype(BF16)
        send(("DZB",), SB, RZB, dz=1)

    lane = lax.broadcasted_iota(jnp.int32, (64, 128), 1)

    def teacher():
        load_t.wait()
        for half in range(2):
            mine = pl.ds(half * 64, 64)
            v = T[mine, :].astype(F32)
            peak = jnp.max(v, axis=1, keepdims=True)
            e = jnp.exp(v - peak)
            ET[mine, :] = e
            TAB[mine, :] = jnp.where(lane == 0, peak, jnp.sum(e, axis=1, keepdims=True))

    def fin_half(half):
        v = value((0, 0, half))
        parts = []
        if half == 0:
            parts.append((("DZ", 0), RZ.at[0]))
            parts += [(("DYA", dy), RYA.at[dy - 1]) for dy in (1, 3, 2) if (dy, 0, 0) not in DIRECT]
        else:
            parts += [(("DYB", 0, dy), RYB.at[0, dy - 1]) for dy in (1, 3, 2) if (dy, 0, 1) not in DIRECT]
            parts.append((("DZB",), RZB))
        parts += [(("DD", piece), RD.at[k]) for k, piece in enumerate(DIRECT) if piece[2] == half]
        for key, buf in parts:
            arrived(key, buf, dy=1)
            v = v + buf[...].astype(F32)
        mine = pl.ds(half * 64, 64)
        draft_max = jnp.max(v, axis=1, keepdims=True)
        shifted = v - draft_max
        draft_sum = jnp.sum(jnp.exp(shifted), axis=1, keepdims=True)
        table = TAB[mine, :]
        cross = jnp.sum(ET[mine, :] * ((T[mine, :].astype(F32) - table[:, 0:1]) - shifted), axis=1, keepdims=True)
        for k, column in ((2, draft_max), (3, draft_sum), (4, cross)):
            table = jnp.where(lane == k, column, table)
        TAB[mine, :] = table

    def fin0():
        G[t] = jnp.transpose(TAB[...])[0:8, :]
        send(("E0",), G.at[t], G.at[t], dc=1)

    pair = pl.ds((t // 2) * 2, 2)

    def fin1():
        arrived(("E0",), G.at[t], dc=1)
        for j, (dx, dh) in enumerate(CROSS):
            send(("E1",), G.at[pair], G.at[pair], dx=dx, dh=dh)

    def fin2():
        arrived(("E1",), G.at[pl.ds(0, 14)], dx=1)
        tm, ts, dm, ds, cr = (G[:, k, :] for k in range(5))
        tm_all = jnp.max(tm, axis=0, keepdims=True)
        dm_all = jnp.max(dm, axis=0, keepdims=True)
        tw = jnp.exp(tm - tm_all)
        ts_all = jnp.sum(ts * tw, axis=0, keepdims=True)
        ds_all = jnp.sum(ds * jnp.exp(dm - dm_all), axis=0, keepdims=True)
        cr_all = jnp.sum(tw * (cr + ((tm - tm_all) - (dm - dm_all)) * ts), axis=0, keepdims=True)
        out_l[...] = cr_all / ts_all - jnp.log(ts_all) + jnp.log(ds_all)

    teacher()
    st0(0)
    st1(0)
    onward("z", 0)
    onward("down", 0)
    st0(1)
    onward("up", 0)
    st2(0)
    st1(1)
    onward("z", 1)
    onward("down", 1)
    onward("up", 1)
    st0(2)
    onward("z", 2)
    st3(0)
    st2(1)
    st1(2)
    st0(3)
    onward("down", 2)
    onward("up", 2)
    onward("z", 3)
    st4(0)
    st1(3)
    st5(0)
    st2(2)
    st3(1)
    st0(4)
    onward("up", 3)
    st2(3)
    onward("down", 3)
    st6(0)
    st1(4)
    st3(2)
    onward("z", 4)
    st4(1)
    st5(1)
    st6(1)
    st3(3)
    st0(5)
    st2(4)
    st4(2)
    st1(5)
    st0(6)
    st5(2)
    st3(4)
    st6(2)
    st0(7)
    st2(5)
    st4(3)
    st1(6)
    st1(7)
    st5(3)
    st6(3)
    st4(4)
    st5(4)
    st3(5)
    st6(4)
    st2(6)
    st2(7)
    st4(5)
    st3(6)
    st5(5)
    st6(5)
    st4(7)
    st5(7)
    st6(7)
    st4(6)
    st5(6)
    st6(6)
    over_y()
    fin_half(0)
    fin_half(1)
    fin0()
    fin1()
    fin2()
    for copy in sent[-POOL:]:
        copy.wait_send()
    assert len(keys) <= NSEM, len(keys)


def hand_over(joined, loss, out_j, out_l):
    out_j[...] = joined[...]
    out_l[...] = loss[0]


def local(hidden_rows, join_weight, head_weight, teacher_logits):
    vmem = pltpu.VMEM
    n, w, d = len(SLOTS), max(1, len(WIDE)), max(1, len(DIRECT))
    joined, loss = pl.pallas_call(
        kernel,
        out_shape=(jax.ShapeDtypeStruct((64, 2048), BF16), jax.ShapeDtypeStruct((1, 128), F32)),
        in_specs=[pl.BlockSpec(memory_space=pl.ANY)] * 4,
        out_specs=[pl.BlockSpec(memory_space=pltpu.VMEM)] * 2,
        scratch_shapes=[
            vmem((3, 1024, 2048), BF16),
            vmem((2048, 1024), BF16),
            vmem((128, 1024), BF16),
            vmem((16, 3, 64, 1024), BF16),
            vmem((n, 128, 1024), F32),
            vmem((n, 128, 1024), BF16),
            vmem((n, 128, 1024), BF16),
            vmem((n, 3, 128, 256), BF16),
            vmem((n, 3, 128, 256), BF16),
            vmem((n, 128, 256), F32),
            vmem((n, 128, 256), BF16),
            vmem((n, 128, 256), BF16),
            vmem((n, 2, 4, 128, 256), BF16),
            vmem((w, 7, 128, 128), BF16),
            vmem((w, 7, 128, 128), BF16),
            vmem((w, 2, 8, 128, 128), BF16),
            vmem((n, 128, 1024), BF16),
            vmem((4, 64, 1024), BF16),
            vmem((3, 64, 1024), BF16),
            vmem((3, 64, 1024), BF16),
            vmem((2, 3, 64, 1024), BF16),
            vmem((64, 1024), BF16),
            vmem((64, 1024), BF16),
            vmem((d, 64, 1024), BF16),
            vmem((128, 1024), F32),
            vmem((128, 128), F32),
            vmem((16, 8, 128), F32),
            pltpu.SemaphoreType.DMA((7,)),
            pltpu.SemaphoreType.DMA((POOL,)),
            pltpu.SemaphoreType.DMA((NSEM,)),
        ],
        compiler_params=pltpu.CompilerParams(
            collective_id=0, has_side_effects=True, vmem_limit_bytes=60 * 1024 * 1024
        ),
        cost_estimate=pl.CostEstimate(flops=17179869184, bytes_accessed=18350080, transcendentals=262144),
    )(hidden_rows, join_weight, head_weight, teacher_logits)
    return pl.pallas_call(
        hand_over,
        out_shape=(jax.ShapeDtypeStruct((64, 2048), BF16), jax.ShapeDtypeStruct((128,), F32)),
        in_specs=[pl.BlockSpec(memory_space=pltpu.VMEM)] * 2,
        out_specs=[pl.BlockSpec(memory_space=pltpu.VMEM)] * 2,
    )(joined, loss)


def solution(mesh):
    in_specs = (P(None, "grp", "tp"), P(None, "tp", "grp"), P("grp", "tp"), P("grp", "tp"))
    out_specs = (P("tp", "grp"), P("grp"))
    return jax.shard_map(local, mesh=mesh, in_specs=in_specs, out_specs=out_specs, check_vma=False)
```

```python
import jax
import jax.numpy as jnp
from jax import lax
from jax.experimental import pallas as pl
from jax.experimental.pallas import tpu as pltpu
from jax.sharding import PartitionSpec as P

MESH = pl.DeviceIdType.MESH
F32 = jnp.float32
BF16 = jnp.bfloat16

SLOTS = (
    ((0, 0, 0), (0, 0, 1)),
    ((3, 0, 1), (1, 0, 1)),
    ((0, 1, 0), (3, 0, 0)),
    ((1, 1, 0), (3, 1, 1)),
    ((2, 0, 0), (2, 0, 1)),
    ((1, 1, 1), (3, 1, 0)),
    ((2, 1, 0), (0, 1, 1)),
    ((2, 1, 1), (1, 0, 0)),
)
WIDE = (7,)
DIRECT = (
    (2, 1, 0),
    (2, 0, 0),
    (2, 1, 1),
)
PLACE = {piece: (s, pos) for s, slot in enumerate(SLOTS) for pos, piece in enumerate(slot)}

START = (
    ("up", (0, 0, 1), (0, 64)),
    ("down", (0, 0, 1), (0, 64)),
    ("z", (0, 0, 0), (0, 64)),
    ("up", (0, 0, 0), (0, 64)),
    ("down", (0, 0, 0), (0, 32)),
    ("z", (0, 0, 1), (0, 16)),
)
LATER = {
    "up": (("up", (0, 1, 0), (0, 32)), ("up", (3, 0, 0), (0, 64)), ("up", (0, 1, 0), (32, 32)), ("up", (3, 1, 1), (0, 64))),
    "down": (("down", (0, 1, 0), (0, 64)), ("down", (1, 0, 1), (0, 64)), ("down", (1, 1, 0), (0, 64)), ("down", (0, 0, 0), (32, 32))),
    "z": (("z", (3, 0, 1), (0, 16)), ("z", (3, 0, 1), (16, 16)), ("z", (3, 0, 1), (32, 16)), ("z", (3, 0, 1), (48, 16)), ("z", (1, 0, 1), (0, 16)), ("z", (1, 0, 1), (16, 16)), ("z", (1, 0, 1), (32, 16)), ("z", (1, 0, 1), (48, 16)), ("z", (0, 0, 1), (16, 16)), ("z", (0, 0, 1), (32, 16)), ("z", (0, 0, 1), (48, 16))),
}
TO = {"up": dict(dy=1), "down": dict(dy=3), "z": dict(dz=1)}


def lands(copy):
    way, (dy, dz, half), _ = copy
    return (dy + {"up": 3, "down": 1, "z": 0}[way]) % 4, dz ^ (way == "z"), half


COPIES = START + sum(LATER.values(), ())
CROSS = ((2, 1), (1, 1), (3, 1), (0, 1), (2, 0), (1, 0), (3, 0))
NSEM = 104
POOL = 48


def kernel(
    hid, wj, wh, tl, out_j, out_l,
    W, H, T, X, ACC, S0, R0, S1, R1, Q, S2, R2, JS, S8, R8, J8, LS, RZ, SA, RYA, RYB, SB, RZB, RD,
    ET, TAB, G, loc, snd, rcv,
):
    g = lax.axis_index("grp")
    t = lax.axis_index("tp")
    y, zl = g // 2, g % 2
    zh, x, c = t // 8, (t // 2) % 4, t % 2

    def dev(dy=0, dz=0, dx=0, dh=0, dc=0):
        return (
            lax.rem(y + dy, 4) * 2 + lax.rem(zl + dz, 2),
            lax.rem(zh + dh, 2) * 8 + lax.rem(x + dx, 4) * 2 + lax.rem(c + dc, 2),
        )

    def pid(piece):
        dy, dz, half = piece
        return (lax.rem(y + dy, 4) * 2 + lax.rem(zl + dz, 2)) * 2 + half

    keys = {}
    sent = []

    def remote(key, src, dst, turn, **to):
        k = keys.setdefault(key, len(keys))
        return pltpu.make_async_remote_copy(
            src_ref=src, dst_ref=dst, send_sem=snd.at[turn], recv_sem=rcv.at[k],
            device_id=dev(**to), device_id_type=MESH,
        )

    def send(key, src, dst, **to):
        if len(sent) >= POOL:
            sent[-POOL].wait_send()
        copy = remote(key, src, dst, len(sent) % POOL, **to)
        copy.start()
        sent.append(copy)

    def arrived(key, dst, **to):
        remote(key, dst, dst, 0, **to).wait_recv()

    def own_rows(half):
        return pltpu.make_async_copy(
            hid.at[:, pl.ds(half * 64, 64), :], X.at[pid((0, 0, half))], loc.at[half]
        )

    loads = [pltpu.make_async_copy(wj.at[l], W.at[l], loc.at[2 + l]) for l in range(3)]
    load_h = pltpu.make_async_copy(wh, H, loc.at[5])
    load_t = pltpu.make_async_copy(tl, T, loc.at[6])

    peers = (
        [dict(dy=k) for k in (1, 2, 3)] + [dict(dz=1), dict(dc=1)]
        + [dict(dx=k, dh=h, dc=i) for k, h in CROSS for i in range(2)] + [dict(dy=k, dz=1) for k in (2,)]
    )
    barrier = pltpu.get_barrier_semaphore()
    for to in peers:
        pl.semaphore_signal(barrier, inc=1, device_id=dev(**to), device_id_type=MESH)
    own_rows(0).start()
    own_rows(1).start()
    for load in loads:
        load.start()
    load_t.start()
    load_h.start()
    pl.semaphore_wait(barrier, len(peers))

    def rows(piece, part):
        return X.at[pid(piece), :, pl.ds(*part), :]

    waited = set()

    def need(piece, part=(0, 64)):
        for copy in COPIES:
            first, count = copy[2]
            meets = first < part[0] + part[1] and part[0] < first + count
            if lands(copy) == piece and meets and copy not in waited:
                waited.add(copy)
                arrived(copy, rows(piece, copy[2]), **TO[copy[0]])

    def move(copy):
        way, piece, part = copy
        if piece[:2] == (0, 0):
            src = hid.at[:, pl.ds(piece[2] * 64 + part[0], part[1]), :]
        else:
            need(piece, part)
            src = rows(piece, part)
        send(copy, src, rows(piece, part), **TO[way])

    def onward(way, k):
        move(LATER[way][k])

    for copy in START:
        move(copy)

    def size(s):
        return 64 * len(SLOTS[s])

    def top(s):
        return pl.ds(0, size(s))

    def joined(s, core):
        places = [pid(piece) for piece in SLOTS[s]]
        cols = pl.ds(pl.multiple_of(core * 1024, 1024), 1024)
        total = None
        for l in range(3):
            a = jnp.concatenate([X[p, l] for p in places], axis=0)
            part = jnp.dot(a, W[l, :, cols], preferred_element_type=F32)
            total = part if total is None else total + part
        return total

    def st0(s):
        for piece in SLOTS[s]:
            need(piece)
        if s == 0:
            own_rows(0).wait()
            own_rows(1).wait()
            for load in loads:
                load.wait()
        S0[s, top(s)] = joined(s, 1 - c).astype(BF16)
        send(("B0", s), S0.at[s, top(s)], R0.at[s, top(s)], dc=1)

    def st9(s):
        ACC[s, top(s)] = joined(s, c)

    def pair_sum(s, first, count):
        cols = pl.ds(pl.multiple_of(first, count), count)
        return ACC[s, top(s), cols] + R0[s, top(s), cols].astype(F32)

    def st1(s):
        arrived(("B0", s), R0.at[s, top(s)], dc=1)
        if s in WIDE:
            w = WIDE.index(s)
            for j, (dx, dh) in enumerate(CROSS):
                S8[w, j, top(s)] = pair_sum(s, (lax.rem(zh + dh, 2) * 4 + lax.rem(x + dx, 4)) * 128, 128).astype(BF16)
                send(("B1", s), S8.at[w, j, top(s)], R8.at[w, j, top(s)], dx=dx, dh=dh)
            Q[s, top(s), 0:128] = pair_sum(s, (zh * 4 + x) * 128, 128)
            return
        for j in (2, 1, 3):
            S1[s, j - 1, top(s)] = pair_sum(s, lax.rem(x + j, 4) * 256, 256).astype(BF16)
            send(("B1", s), S1.at[s, j - 1, top(s)], R1.at[s, j - 1, top(s)], dx=j)
        Q[s, top(s)] = pair_sum(s, x * 256, 256)

    def st2(s):
        if s in WIDE:
            w = WIDE.index(s)
            v = Q[s, top(s), 0:128]
            arrived(("B1", s), R8.at[w, :, top(s)], dx=1)
            for j in range(7):
                v = v + R8[w, j, top(s)].astype(F32)
            mine = J8.at[w, c, zh * 4 + x, top(s)]
            mine[...] = v.astype(BF16)
            for j, (dx, dh) in enumerate(CROSS):
                send(("C1", s), mine, mine, dx=dx, dh=dh)
            return
        v = Q[s, top(s)]
        arrived(("B1", s), R1.at[s, :, top(s)], dx=1)
        for j in (1, 2, 3):
            v = v + R1[s, j - 1, top(s)].astype(F32)
        S2[s, top(s)] = v.astype(BF16)
        send(("B2", s), S2.at[s, top(s)], R2.at[s, top(s)], dh=1)

    def st3(s):
        arrived(("B2", s), R2.at[s, top(s)], dh=1)
        mine = JS.at[s, c, x, top(s)]
        mine[...] = (S2[s, top(s)].astype(F32) + R2[s, top(s)].astype(F32)).astype(BF16)
        for j in (2, 1, 3):
            send(("C1", s), mine, mine, dx=j)

    def blocks(s):
        if s in WIDE:
            return J8, WIDE.index(s), 8
        return JS, s, 4

    def st4(s):
        buf, k, parts = blocks(s)
        arrived(("C1", s), buf.at[k, c, pl.ds(0, parts - 1), top(s)], dx=1)
        send(("C0", s), buf.at[k, c, :, top(s)], buf.at[k, c, :, top(s)], dc=1)

    def st5(s):
        if s == 0:
            load_h.wait()
        buf, k, parts = blocks(s)
        arrived(("C0", s), buf.at[k, 1 - c, :, top(s)], dc=1)
        cuts = [(i, j) for i in range(2) for j in range(parts)]

        a = jnp.concatenate([buf[k, i, j, top(s)] for i, j in cuts], axis=1)
        LS[s, top(s)] = jnp.dot(a, H[...], preferred_element_type=F32).astype(BF16)

    def logits(piece):
        s, pos = PLACE[piece]
        return LS.at[s, pl.ds(pos * 64, 64), :]

    def value(piece):
        s, pos = PLACE[piece]
        return LS[s, pos * 64 : pos * 64 + 64, :].astype(F32)

    def st6(s):
        for piece in SLOTS[s]:
            dy, dz, half = piece
            if piece in DIRECT:
                send(("DD", piece), logits(piece), RD.at[DIRECT.index(piece)], dy=dy, dz=dz)
            elif half == 0 and dz == 1:
                send(("DZ", dy), logits(piece), RZ.at[dy], dz=1)
            elif half == 1 and dy != 0:
                send(("DYB", dz, dy), logits(piece), RYB.at[dz, dy - 1], dy=dy)
        for pos, piece in enumerate(SLOTS[s]):
            buf, k, parts = blocks(s)

            @pl.when(pid(piece) == t)
            def _():
                width = 1024 // parts
                for i in range(2):
                    for j in range(parts):
                        col = i * 1024 + j * width
                        out_j[:, col : col + width] = buf[k, i, j, pos * 64 : pos * 64 + 64, :]

    def over_z(dy):
        arrived(("DZ", dy), RZ.at[dy], dz=1)
        SA[dy - 1] = (value((dy, 0, 0)) + RZ[dy].astype(F32)).astype(BF16)
        send(("DYA", dy), SA.at[dy - 1], RYA.at[dy - 1], dy=dy)

    def over_y():
        v = value((0, 1, 1))
        for dy in (1, 3, 2):
            if (dy, 1, 1) not in DIRECT:
                arrived(("DYB", 1, dy), RYB.at[1, dy - 1], dy=dy)
                v = v + RYB[1, dy - 1].astype(F32)
        SB[...] = v.astype(BF16)
        send(("DZB",), SB, RZB, dz=1)

    lane = lax.broadcasted_iota(jnp.int32, (64, 128), 1)

    def teacher():
        load_t.wait()
        for half in range(2):
            mine = pl.ds(half * 64, 64)
            v = T[mine, :].astype(F32)
            peak = jnp.max(v, axis=1, keepdims=True)
            e = jnp.exp(v - peak)
            ET[mine, :] = e
            TAB[mine, :] = jnp.where(lane == 0, peak, jnp.sum(e, axis=1, keepdims=True))

    def fin_half(half):
        v = value((0, 0, half))
        parts = []
        if half == 0:
            parts.append((("DZ", 0), RZ.at[0]))
            parts += [(("DYA", dy), RYA.at[dy - 1]) for dy in (1, 3, 2) if (dy, 0, 0) not in DIRECT]
        else:
            parts += [(("DYB", 0, dy), RYB.at[0, dy - 1]) for dy in (1, 3, 2) if (dy, 0, 1) not in DIRECT]
            parts.append((("DZB",), RZB))
        parts += [(("DD", piece), RD.at[k]) for k, piece in enumerate(DIRECT) if piece[2] == half]
        for key, buf in parts:
            arrived(key, buf, dy=1)
            v = v + buf[...].astype(F32)
        mine = pl.ds(half * 64, 64)
        draft_max = jnp.max(v, axis=1, keepdims=True)
        shifted = v - draft_max
        draft_sum = jnp.sum(jnp.exp(shifted), axis=1, keepdims=True)
        table = TAB[mine, :]
        cross = jnp.sum(ET[mine, :] * ((T[mine, :].astype(F32) - table[:, 0:1]) - shifted), axis=1, keepdims=True)
        for k, column in ((2, draft_max), (3, draft_sum), (4, cross)):
            table = jnp.where(lane == k, column, table)
        TAB[mine, :] = table

    def fin0():
        G[t] = jnp.transpose(TAB[...])[0:8, :]
        for dx, dh in CROSS:
            for dc in (1, 0):
                send(("E",), G.at[t], G.at[t], dx=dx, dh=dh, dc=dc)
        send(("E",), G.at[t], G.at[t], dc=1)

    def fin2():
        arrived(("E",), G.at[pl.ds(0, 15)], dc=1)
        tm, ts, dm, ds, cr = (G[:, k, :] for k in range(5))
        tm_all = jnp.max(tm, axis=0, keepdims=True)
        dm_all = jnp.max(dm, axis=0, keepdims=True)
        tw = jnp.exp(tm - tm_all)
        ts_all = jnp.sum(ts * tw, axis=0, keepdims=True)
        ds_all = jnp.sum(ds * jnp.exp(dm - dm_all), axis=0, keepdims=True)
        cr_all = jnp.sum(tw * (cr + ((tm - tm_all) - (dm - dm_all)) * ts), axis=0, keepdims=True)
        out_l[...] = cr_all / ts_all - jnp.log(ts_all) + jnp.log(ds_all)

    st0(0)
    st9(0)
    teacher()
    st1(0)
    st2(0)
    onward("down", 0)
    st0(1)
    onward("z", 0)
    onward("z", 1)
    st9(1)
    st1(1)
    st3(0)
    onward("up", 0)
    onward("z", 2)
    onward("z", 3)
    onward("down", 1)
    st2(1)
    onward("up", 1)
    st0(2)
    st9(2)
    st4(0)
    st1(2)
    onward("z", 4)
    onward("z", 5)
    st5(0)
    st0(3)
    st9(3)
    onward("z", 6)
    st3(1)
    st1(3)
    st2(2)
    onward("down", 2)
    onward("up", 2)
    onward("z", 7)
    onward("z", 8)
    onward("up", 3)
    st4(1)
    st5(1)
    st3(2)
    onward("z", 9)
    st0(4)
    st2(3)
    st9(4)
    st1(4)
    onward("z", 10)
    onward("down", 3)
    st0(5)
    st9(5)
    st4(2)
    st1(5)
    st6(1)
    st6(0)
    st5(2)
    st3(3)
    st2(4)
    st6(2)
    st0(6)
    st9(6)
    st2(5)
    st1(6)
    st0(7)
    st3(4)
    st9(7)
    st1(7)
    st4(3)
    st5(3)
    st2(6)
    st6(3)
    st3(5)
    st4(4)
    st5(4)
    st6(4)
    st3(6)
    st2(7)
    st4(5)
    st5(5)
    st6(5)
    st4(6)
    st5(6)
    st6(6)
    st4(7)
    st5(7)
    st6(7)
    over_z(1)
    over_z(3)
    over_y()
    fin_half(1)
    fin_half(0)
    fin0()
    fin2()
    for copy in sent[-POOL:]:
        copy.wait_send()
    assert len(keys) <= NSEM, len(keys)


def hand_over(joined, loss, out_j, out_l):
    out_j[...] = joined[...]
    out_l[...] = loss[0]


def local(hidden_rows, join_weight, head_weight, teacher_logits):
    vmem = pltpu.VMEM
    n, w, d = len(SLOTS), max(1, len(WIDE)), max(1, len(DIRECT))
    joined, loss = pl.pallas_call(
        kernel,
        out_shape=(jax.ShapeDtypeStruct((64, 2048), BF16), jax.ShapeDtypeStruct((1, 128), F32)),
        in_specs=[pl.BlockSpec(memory_space=pl.ANY)] * 4,
        out_specs=[pl.BlockSpec(memory_space=pltpu.VMEM)] * 2,
        scratch_shapes=[
            vmem((3, 1024, 2048), BF16),
            vmem((2048, 1024), BF16),
            vmem((128, 1024), BF16),
            vmem((16, 3, 64, 1024), BF16),
            vmem((n, 128, 1024), F32),
            vmem((n, 128, 1024), BF16),
            vmem((n, 128, 1024), BF16),
            vmem((n, 3, 128, 256), BF16),
            vmem((n, 3, 128, 256), BF16),
            vmem((n, 128, 256), F32),
            vmem((n, 128, 256), BF16),
            vmem((n, 128, 256), BF16),
            vmem((n, 2, 4, 128, 256), BF16),
            vmem((w, 7, 128, 128), BF16),
            vmem((w, 7, 128, 128), BF16),
            vmem((w, 2, 8, 128, 128), BF16),
            vmem((n, 128, 1024), BF16),
            vmem((4, 64, 1024), BF16),
            vmem((3, 64, 1024), BF16),
            vmem((3, 64, 1024), BF16),
            vmem((2, 3, 64, 1024), BF16),
            vmem((64, 1024), BF16),
            vmem((64, 1024), BF16),
            vmem((d, 64, 1024), BF16),
            vmem((128, 1024), F32),
            vmem((128, 128), F32),
            vmem((16, 8, 128), F32),
            pltpu.SemaphoreType.DMA((7,)),
            pltpu.SemaphoreType.DMA((POOL,)),
            pltpu.SemaphoreType.DMA((NSEM,)),
        ],
        compiler_params=pltpu.CompilerParams(
            collective_id=0, has_side_effects=True, vmem_limit_bytes=60 * 1024 * 1024
        ),
        cost_estimate=pl.CostEstimate(flops=17179869184, bytes_accessed=18350080, transcendentals=262144),
    )(hidden_rows, join_weight, head_weight, teacher_logits)
    return pl.pallas_call(
        hand_over,
        out_shape=(jax.ShapeDtypeStruct((64, 2048), BF16), jax.ShapeDtypeStruct((128,), F32)),
        in_specs=[pl.BlockSpec(memory_space=pltpu.VMEM)] * 2,
        out_specs=[pl.BlockSpec(memory_space=pltpu.VMEM)] * 2,
    )(joined, loss)


def solution(mesh):
    in_specs = (P(None, "grp", "tp"), P(None, "tp", "grp"), P("grp", "tp"), P("grp", "tp"))
    out_specs = (P("tp", "grp"), P("grp"))
    return jax.shard_map(local, mesh=mesh, in_specs=in_specs, out_specs=out_specs, check_vma=False)
```

```python
import jax
import jax.numpy as jnp
from jax import lax
from jax.experimental import pallas as pl
from jax.experimental.pallas import tpu as pltpu
from jax.sharding import PartitionSpec as P

MESH = pl.DeviceIdType.MESH
F32 = jnp.float32
BF16 = jnp.bfloat16

SLOTS = (
    ((0, 0, 0), (0, 0, 1)),
    ((3, 0, 1), (1, 0, 1)),
    ((0, 1, 0), (3, 0, 0)),
    ((1, 1, 0), (3, 1, 1)),
    ((2, 0, 0), (2, 0, 1)),
    ((1, 1, 1), (3, 1, 0)),
    ((2, 1, 0), (0, 1, 1)),
    ((2, 1, 1), (1, 0, 0)),
)
WIDE = (7,)
DIRECT = (
    (2, 1, 0),
    (2, 0, 0),
    (2, 1, 1),
)
PLACE = {piece: (s, pos) for s, slot in enumerate(SLOTS) for pos, piece in enumerate(slot)}

START = (
    ("up", (0, 0, 1), (0, 64)),
    ("down", (0, 0, 1), (0, 64)),
    ("z", (0, 0, 0), (0, 64)),
    ("up", (0, 0, 0), (0, 64)),
    ("down", (0, 0, 0), (0, 32)),
    ("z", (0, 0, 1), (0, 16)),
)
LATER = {
    "up": (("up", (0, 1, 0), (0, 32)), ("up", (3, 0, 0), (0, 64)), ("up", (0, 1, 0), (32, 32)), ("up", (3, 1, 1), (0, 64))),
    "down": (("down", (0, 1, 0), (0, 64)), ("down", (1, 0, 1), (0, 64)), ("down", (1, 1, 0), (0, 64)), ("down", (0, 0, 0), (32, 32))),
    "z": (("z", (3, 0, 1), (0, 16)), ("z", (3, 0, 1), (16, 16)), ("z", (3, 0, 1), (32, 16)), ("z", (3, 0, 1), (48, 16)), ("z", (1, 0, 1), (0, 16)), ("z", (1, 0, 1), (16, 16)), ("z", (1, 0, 1), (32, 16)), ("z", (1, 0, 1), (48, 16)), ("z", (0, 0, 1), (16, 16)), ("z", (0, 0, 1), (32, 16)), ("z", (0, 0, 1), (48, 16))),
}
TO = {"up": dict(dy=1), "down": dict(dy=3), "z": dict(dz=1)}


def lands(copy):
    way, (dy, dz, half), _ = copy
    return (dy + {"up": 3, "down": 1, "z": 0}[way]) % 4, dz ^ (way == "z"), half


COPIES = START + sum(LATER.values(), ())
CROSS = ((2, 1), (1, 1), (3, 1), (0, 1), (2, 0), (1, 0), (3, 0))
NSEM = 80
POOL = 40


def kernel(
    hid, wj, wh, tl, out_j, out_l,
    W, H, T, X, ACC, S0, R0, S1, R1, Q, S2, R2, JS, S8, R8, J8, LS, RZ, SA, RYA, RYB, SB, RZB, RD,
    ET, TAB, G, J, loc, snd, rcv,
):
    g = lax.axis_index("grp")
    t = lax.axis_index("tp")
    y, zl = g // 2, g % 2
    zh, x, c = t // 8, (t // 2) % 4, t % 2

    def dev(dy=0, dz=0, dx=0, dh=0, dc=0):
        return (
            lax.rem(y + dy, 4) * 2 + lax.rem(zl + dz, 2),
            lax.rem(zh + dh, 2) * 8 + lax.rem(x + dx, 4) * 2 + lax.rem(c + dc, 2),
        )

    def pid(piece):
        dy, dz, half = piece
        return (lax.rem(y + dy, 4) * 2 + lax.rem(zl + dz, 2)) * 2 + half

    keys = {}
    sent = []

    def remote(key, src, dst, turn, **to):
        k = keys.setdefault(key, len(keys))
        return pltpu.make_async_remote_copy(
            src_ref=src, dst_ref=dst, send_sem=snd.at[turn], recv_sem=rcv.at[k],
            device_id=dev(**to), device_id_type=MESH,
        )

    def send(key, src, dst, **to):
        if len(sent) >= POOL:
            sent[-POOL].wait_send()
        copy = remote(key, src, dst, len(sent) % POOL, **to)
        copy.start()
        sent.append(copy)

    def arrived(key, dst, **to):
        remote(key, dst, dst, 0, **to).wait_recv()

    def own_rows(half):
        return pltpu.make_async_copy(
            hid.at[:, pl.ds(half * 64, 64), :], X.at[pid((0, 0, half))], loc.at[half]
        )

    loads = [pltpu.make_async_copy(wj.at[l], W.at[l], loc.at[2 + l]) for l in range(3)]
    load_h = pltpu.make_async_copy(wh, H, loc.at[5])
    load_t = pltpu.make_async_copy(tl, T, loc.at[6])

    peers = (
        [dict(dy=1), dict(dy=3), dict(dz=1), dict(dc=1), dict(dh=1)] + [dict(dx=k) for k in (1, 2, 3)]
    )
    barrier = pltpu.get_barrier_semaphore()
    for to in peers:
        pl.semaphore_signal(barrier, inc=1, device_id=dev(**to), device_id_type=MESH)
    own_rows(0).start()
    own_rows(1).start()
    for load in loads:
        load.start()
    load_t.start()
    load_h.start()
    pl.semaphore_wait(barrier, len(peers))

    def rows(piece, part):
        return X.at[pid(piece), :, pl.ds(*part), :]

    waited = set()

    def need(piece, part=(0, 64)):
        for copy in COPIES:
            first, count = copy[2]
            meets = first < part[0] + part[1] and part[0] < first + count
            if lands(copy) == piece and meets and copy not in waited:
                waited.add(copy)
                arrived(copy, rows(piece, copy[2]), **TO[copy[0]])

    def move(copy):
        way, piece, part = copy
        if piece[:2] == (0, 0):
            src = hid.at[:, pl.ds(piece[2] * 64 + part[0], part[1]), :]
        else:
            need(piece, part)
            src = rows(piece, part)
        send(copy, src, rows(piece, part), **TO[way])

    def onward(way, k):
        move(LATER[way][k])

    for copy in START:
        move(copy)

    def size(s):
        return 64 * len(SLOTS[s])

    def top(s):
        return pl.ds(0, size(s))

    def joined(s, core):
        places = [pid(piece) for piece in SLOTS[s]]
        cols = pl.ds(pl.multiple_of(core * 1024, 1024), 1024)
        total = None
        for l in range(3):
            a = jnp.concatenate([X[p, l] for p in places], axis=0)
            part = jnp.dot(a, W[l, :, cols], preferred_element_type=F32)
            total = part if total is None else total + part
        return total

    def st0(s):
        for piece in SLOTS[s]:
            need(piece)
        if s == 0:
            own_rows(0).wait()
            own_rows(1).wait()
            for load in loads:
                load.wait()
        S0[s, top(s)] = joined(s, 1 - c).astype(BF16)
        send(("B0", s), S0.at[s, top(s)], R0.at[s, top(s)], dc=1)

    def st9(s):
        ACC[s, top(s)] = joined(s, c)

    def pair_sum(s, first, count):
        cols = pl.ds(pl.multiple_of(first, count), count)
        return ACC[s, top(s), cols] + R0[s, top(s), cols].astype(F32)

    def st1(s):
        arrived(("B0", s), R0.at[s, top(s)], dc=1)
        if s in WIDE:
            w = WIDE.index(s)
            for j, (dx, dh) in enumerate(CROSS):
                S8[w, j, top(s)] = pair_sum(s, (lax.rem(zh + dh, 2) * 4 + lax.rem(x + dx, 4)) * 128, 128).astype(BF16)
                send(("B1", s), S8.at[w, j, top(s)], R8.at[w, j, top(s)], dx=dx, dh=dh)
            Q[s, top(s), 0:128] = pair_sum(s, (zh * 4 + x) * 128, 128)
            return
        for j in (2, 1, 3):
            S1[s, j - 1, top(s)] = pair_sum(s, lax.rem(x + j, 4) * 256, 256).astype(BF16)
            send(("B1", s), S1.at[s, j - 1, top(s)], R1.at[s, j - 1, top(s)], dx=j)
        Q[s, top(s)] = pair_sum(s, x * 256, 256)

    def st2(s):
        if s in WIDE:
            w = WIDE.index(s)
            v = Q[s, top(s), 0:128]
            arrived(("B1", s), R8.at[w, :, top(s)], dx=1)
            for j in range(7):
                v = v + R8[w, j, top(s)].astype(F32)
            mine = J8.at[w, c, zh * 4 + x, top(s)]
            mine[...] = v.astype(BF16)
            for j, (dx, dh) in enumerate(CROSS):
                send(("C1", s), mine, mine, dx=dx, dh=dh)
            return
        v = Q[s, top(s)]
        arrived(("B1", s), R1.at[s, :, top(s)], dx=1)
        for j in (1, 2, 3):
            v = v + R1[s, j - 1, top(s)].astype(F32)
        S2[s, top(s)] = v.astype(BF16)
        send(("B2", s), S2.at[s, top(s)], R2.at[s, top(s)], dh=1)

    def st3(s):
        arrived(("B2", s), R2.at[s, top(s)], dh=1)
        mine = JS.at[s, c, x, top(s)]
        mine[...] = (S2[s, top(s)].astype(F32) + R2[s, top(s)].astype(F32)).astype(BF16)
        for j in (2, 1, 3):
            send(("C1", s), mine, mine, dx=j)

    def blocks(s):
        if s in WIDE:
            return J8, WIDE.index(s), 8
        return JS, s, 4

    def st4(s):
        buf, k, parts = blocks(s)
        arrived(("C1", s), buf.at[k, c, pl.ds(0, parts - 1), top(s)], dx=1)
        send(("C0", s), buf.at[k, c, :, top(s)], buf.at[k, c, :, top(s)], dc=1)

    def st5(s):
        if s == 0:
            load_h.wait()
        buf, k, parts = blocks(s)
        arrived(("C0", s), buf.at[k, 1 - c, :, top(s)], dc=1)
        cuts = [(i, j) for i in range(2) for j in range(parts)]

        a = jnp.concatenate([buf[k, i, j, top(s)] for i, j in cuts], axis=1)
        LS[s, top(s)] = jnp.dot(a, H[...], preferred_element_type=F32).astype(BF16)

    def logits(piece):
        s, pos = PLACE[piece]
        return LS.at[s, pl.ds(pos * 64, 64), :]

    def value(piece):
        s, pos = PLACE[piece]
        return LS[s, pos * 64 : pos * 64 + 64, :].astype(F32)

    def st6(s):
        for piece in SLOTS[s]:
            dy, dz, half = piece
            if piece in DIRECT:
                send(("DD", piece), logits(piece), RD.at[DIRECT.index(piece)], dy=dy, dz=dz)
            elif half == 0 and dz == 1:
                send(("DZ", dy), logits(piece), RZ.at[dy], dz=1)
            elif half == 1 and dy != 0:
                send(("DYB", dz, dy), logits(piece), RYB.at[dz, dy - 1], dy=dy)
        for pos, piece in enumerate(SLOTS[s]):
            buf, k, parts = blocks(s)

            @pl.when(pid(piece) == t)
            def _():
                width = 1024 // parts
                for i in range(2):
                    for j in range(parts):
                        col = i * 1024 + j * width
                        J[:, col : col + width] = buf[k, i, j, pos * 64 : pos * 64 + 64, :]

    def over_z(dy):
        arrived(("DZ", dy), RZ.at[dy], dz=1)
        SA[dy - 1] = (value((dy, 0, 0)) + RZ[dy].astype(F32)).astype(BF16)
        send(("DYA", dy), SA.at[dy - 1], RYA.at[dy - 1], dy=dy)

    def over_y():
        v = value((0, 1, 1))
        for dy in (1, 3, 2):
            if (dy, 1, 1) not in DIRECT:
                arrived(("DYB", 1, dy), RYB.at[1, dy - 1], dy=dy)
                v = v + RYB[1, dy - 1].astype(F32)
        SB[...] = v.astype(BF16)
        send(("DZB",), SB, RZB, dz=1)

    hand_j = pltpu.make_async_copy(J, out_j, loc.at[0])

    lane = lax.broadcasted_iota(jnp.int32, (64, 128), 1)

    def teacher():
        load_t.wait()
        for half in range(2):
            mine = pl.ds(half * 64, 64)
            v = T[mine, :].astype(F32)
            peak = jnp.max(v, axis=1, keepdims=True)
            e = jnp.exp(v - peak)
            ET[mine, :] = e
            TAB[mine, :] = jnp.where(lane == 0, peak, jnp.sum(e, axis=1, keepdims=True))

    def fin_half(half):
        v = value((0, 0, half))
        parts = []
        if half == 0:
            parts.append((("DZ", 0), RZ.at[0]))
            parts += [(("DYA", dy), RYA.at[dy - 1]) for dy in (1, 3, 2) if (dy, 0, 0) not in DIRECT]
        else:
            parts += [(("DYB", 0, dy), RYB.at[0, dy - 1]) for dy in (1, 3, 2) if (dy, 0, 1) not in DIRECT]
            parts.append((("DZB",), RZB))
        parts += [(("DD", piece), RD.at[k]) for k, piece in enumerate(DIRECT) if piece[2] == half]
        for key, buf in parts:
            arrived(key, buf, dy=1)
            v = v + buf[...].astype(F32)
        mine = pl.ds(half * 64, 64)
        draft_max = jnp.max(v, axis=1, keepdims=True)
        shifted = v - draft_max
        draft_sum = jnp.sum(jnp.exp(shifted), axis=1, keepdims=True)
        table = TAB[mine, :]
        cross = jnp.sum(ET[mine, :] * ((T[mine, :].astype(F32) - table[:, 0:1]) - shifted), axis=1, keepdims=True)
        for k, column in ((2, draft_max), (3, draft_sum), (4, cross)):
            table = jnp.where(lane == k, column, table)
        TAB[mine, :] = table

    def fin0():
        G[t] = jnp.transpose(TAB[...])[0:8, :]
        for dx, dh in CROSS:
            for dc in (1, 0):
                send(("E",), G.at[t], G.at[t], dx=dx, dh=dh, dc=dc)
        send(("E",), G.at[t], G.at[t], dc=1)

    def fin2():
        arrived(("E",), G.at[pl.ds(0, 15)], dc=1)
        tm, ts, dm, ds, cr = (G[:, k, :] for k in range(5))
        tm_all = jnp.max(tm, axis=0, keepdims=True)
        dm_all = jnp.max(dm, axis=0, keepdims=True)
        tw = jnp.exp(tm - tm_all)
        ts_all = jnp.sum(ts * tw, axis=0, keepdims=True)
        ds_all = jnp.sum(ds * jnp.exp(dm - dm_all), axis=0, keepdims=True)
        cr_all = jnp.sum(tw * (cr + ((tm - tm_all) - (dm - dm_all)) * ts), axis=0, keepdims=True)
        out_l[...] = cr_all / ts_all - jnp.log(ts_all) + jnp.log(ds_all)

    st0(0)
    st9(0)
    teacher()
    st1(0)
    st2(0)
    onward("down", 0)
    onward("z", 0)
    st0(1)
    st9(1)
    onward("z", 1)
    onward("z", 2)
    st1(1)
    onward("up", 0)
    st3(0)
    onward("z", 3)
    st2(1)
    onward("up", 1)
    st0(2)
    st9(2)
    onward("z", 4)
    st4(0)
    st1(2)
    onward("down", 1)
    st5(0)
    onward("z", 5)
    st0(3)
    st9(3)
    onward("z", 6)
    st3(1)
    st1(3)
    st2(2)
    onward("down", 2)
    onward("z", 7)
    onward("up", 2)
    onward("z", 8)
    st4(1)
    onward("z", 9)
    st5(1)
    st3(2)
    st0(4)
    st2(3)
    onward("up", 3)
    st9(4)
    st1(4)
    onward("z", 10)
    st0(5)
    st9(5)
    st4(2)
    st1(5)
    onward("down", 3)
    st6(1)
    st6(0)
    st5(2)
    st3(3)
    st2(4)
    st6(2)
    st0(6)
    st9(6)
    st2(5)
    st1(6)
    st3(4)
    st0(7)
    st9(7)
    st4(3)
    st1(7)
    st5(3)
    st3(5)
    st2(6)
    st6(3)
    st4(4)
    st5(4)
    st6(4)
    st3(6)
    st2(7)
    st4(5)
    st5(5)
    st6(5)
    st4(6)
    st5(6)
    st6(6)
    st4(7)
    st5(7)
    st6(7)
    hand_j.start()
    over_z(3)
    over_y()
    over_z(1)
    fin_half(1)
    fin_half(0)
    fin0()
    fin2()
    hand_j.wait()
    for copy in sent[-POOL:]:
        copy.wait_send()
    assert len(keys) <= NSEM, len(keys)


def hand_over(joined, loss, out_j, out_l):
    out_j[...] = joined[...]
    out_l[...] = loss[0]


def local(hidden_rows, join_weight, head_weight, teacher_logits):
    vmem = pltpu.VMEM
    n, w, d = len(SLOTS), max(1, len(WIDE)), max(1, len(DIRECT))
    joined, loss = pl.pallas_call(
        kernel,
        out_shape=(jax.ShapeDtypeStruct((64, 2048), BF16), jax.ShapeDtypeStruct((1, 128), F32)),
        in_specs=[pl.BlockSpec(memory_space=pl.ANY)] * 4,
        out_specs=[pl.BlockSpec(memory_space=pl.ANY), pl.BlockSpec(memory_space=pltpu.VMEM)],
        scratch_shapes=[
            vmem((3, 1024, 2048), BF16),
            vmem((2048, 1024), BF16),
            vmem((128, 1024), BF16),
            vmem((16, 3, 64, 1024), BF16),
            vmem((n, 128, 1024), F32),
            vmem((n, 128, 1024), BF16),
            vmem((n, 128, 1024), BF16),
            vmem((n, 3, 128, 256), BF16),
            vmem((n, 3, 128, 256), BF16),
            vmem((n, 128, 256), F32),
            vmem((n, 128, 256), BF16),
            vmem((n, 128, 256), BF16),
            vmem((n, 2, 4, 128, 256), BF16),
            vmem((w, 7, 128, 128), BF16),
            vmem((w, 7, 128, 128), BF16),
            vmem((w, 2, 8, 128, 128), BF16),
            vmem((n, 128, 1024), BF16),
            vmem((4, 64, 1024), BF16),
            vmem((3, 64, 1024), BF16),
            vmem((3, 64, 1024), BF16),
            vmem((2, 3, 64, 1024), BF16),
            vmem((64, 1024), BF16),
            vmem((64, 1024), BF16),
            vmem((d, 64, 1024), BF16),
            vmem((128, 1024), F32),
            vmem((128, 128), F32),
            vmem((16, 8, 128), F32),
            vmem((64, 2048), BF16),
            pltpu.SemaphoreType.DMA((7,)),
            pltpu.SemaphoreType.DMA((POOL,)),
            pltpu.SemaphoreType.DMA((NSEM,)),
        ],
        compiler_params=pltpu.CompilerParams(
            collective_id=0, has_side_effects=True, vmem_limit_bytes=60 * 1024 * 1024
        ),
        cost_estimate=pl.CostEstimate(flops=17179869184, bytes_accessed=18350080, transcendentals=262144),
    )(hidden_rows, join_weight, head_weight, teacher_logits)
    return pl.pallas_call(
        hand_over,
        out_shape=(jax.ShapeDtypeStruct((64, 2048), BF16), jax.ShapeDtypeStruct((128,), F32)),
        in_specs=[pl.BlockSpec(memory_space=pltpu.VMEM)] * 2,
        out_specs=[pl.BlockSpec(memory_space=pltpu.VMEM)] * 2,
    )(joined, loss)


def solution(mesh):
    in_specs = (P(None, "grp", "tp"), P(None, "tp", "grp"), P("grp", "tp"), P("grp", "tp"))
    out_specs = (P("tp", "grp"), P("grp"))
    return jax.shard_map(local, mesh=mesh, in_specs=in_specs, out_specs=out_specs, check_vma=False)
```
